32 devices in a mesh: src: 2 (over y), dst: 16 (over z, x, core).
Axes of the slice: x: 2, y: 2, z: 4, core: 2. Of those that a mesh axis runs over, the one named last changes fastest.
Arguments:
- node_feats: bfloat16 [512, 256], P(('dst', 'src')), may hold values from -6 to 6
- cotangent: bfloat16 [512, 256], P(('src', 'dst')), may hold values from -6 to 6
- edge_attr: bfloat16 [49152, 128], P(('src', 'dst')), may hold values from -6 to 6
- src_ids: int32 [49152], P(('src', 'dst')), may hold values from 0 to 31
- dst_rel: int32 [49152], P(('src', 'dst')), may hold values from 0 to 127
- offsets: int32 [384], P(('src', 'dst')), may hold values from 0 to 128
- counts: int32 [384], P(('src', 'dst')), may hold values from 32 to 128
- w_node: bfloat16 [256, 512], replicated, may hold values from -0.375 to 0.375
- w_edge: bfloat16 [128, 512], replicated, may hold values from -0.5 to 0.5
- bias: float32 [512], replicated, may hold values from -3 to 3
- w_out: bfloat16 [512, 256], replicated, may hold values from -0.03125 to 0.03125
Outputs:
- aggregated: bfloat16 [512, 256], P(('src', 'dst'))
- node_grads: bfloat16 [512, 256], P(('dst', 'src'))
- attr_grads: bfloat16 [49152, 128], P(('src', 'dst'))
The draws below stay inside these ranges and needn't reach their ends.
Inputs may be any that keep to these rules, and one draw needn't show every extreme that they name: `counts`: slots at or after a block's count carry no edge; their ids are arbitrary within range.
All inputs are finite; a program needn't handle non-finite values.
Results may differ from the reference program's by a relative error of at most 0.0049.
Values may be sent and summed in bfloat16 or wider, within the bound.
No kernel may reach another device: no remote copies, remote signals or barrier semaphores. Data moves between devices by JAX's collectives and lax.ppermute only.
A program may use at most 64 MiB of HBM per device.

```python
import jax
import jax.numpy as jnp
from jax import lax

W = 256
H = 512
EF = 128
BLOCK = 128
NODE_DEV = 16
BLK_DEV = 12
NODES = 512
BLOCKS = 384
EDGES = 49152
N_SRC = 2
N_DST = 16


def place_ends(result, own_key, least, high):
    longest = result.shape.index(max(result.shape))
    spots = []
    for shift in (0, 1):
        where = [jax.random.randint(jax.random.fold_in(own_key, axis), (), 0, length) for axis, length in enumerate(result.shape)]
        where[longest] = (where[longest] + shift) % result.shape[longest]
        spots.append(tuple(where))
    return result.at[spots[0]].set(least).at[spots[1]].set(high)


def shard_levels(rng, shape, shards, low, largest):
    loudness = 1.0
    for axis_at, blocks in shards:
        heights = jax.random.uniform(jax.random.fold_in(jax.random.fold_in(rng, 6), axis_at), (blocks,), jnp.float32, low / len(shards), largest / len(shards))
        loudness = loudness * jnp.repeat(jnp.exp(heights), shape[axis_at] // blocks).reshape((-1,) + (1,) * (len(shape) - 1 - axis_at))
    return loudness


def noise(rng, dims, spread, bound, cuts=(), kind=jnp.bfloat16):
    factor_of = shard_levels(rng, dims, cuts, -0.22, 0.18) if cuts else 1.0
    array = jax.random.normal(rng, dims, jnp.float32) * spread * factor_of
    return jnp.minimum(jnp.maximum(array, -bound), bound).astype(kind)


def setup_inputs(seed: int = 0) -> dict:
    seeds = jax.random.split(jax.random.key(seed), 12)
    node_feats = noise(seeds[0], (NODES, W), 1.0, 6.0, ((0, 32),))
    cotangent = noise(seeds[1], (NODES, W), 1.0, 6.0, ((0, 32),))
    edge_attr = noise(seeds[2], (EDGES, EF), 1.0, 6.0, ((0, 32),))
    src_ids = place_ends(jax.random.randint(seeds[3], (EDGES,), 0, NODE_DEV * N_SRC), jax.random.fold_in(seeds[3], 1), 0, (NODE_DEV * N_SRC) - 1).astype(jnp.int32)
    dst_rel = place_ends(jax.random.randint(seeds[4], (EDGES,), 0, BLOCK), jax.random.fold_in(seeds[4], 1), 0, BLOCK - 1).astype(jnp.int32)
    offsets = place_ends(jax.random.randint(seeds[5], (BLOCKS,), 0, NODE_DEV * N_DST - BLOCK + 1), jax.random.fold_in(seeds[5], 1), 0, NODE_DEV * N_DST - BLOCK).astype(jnp.int32)
    counts = place_ends(jax.random.randint(seeds[6], (BLOCKS,), 32, BLOCK + 1), jax.random.fold_in(seeds[6], 1), 32, BLOCK).astype(jnp.int32)
    w_node = noise(seeds[7], (W, H), W ** -0.5, 0.375)
    w_edge = noise(seeds[8], (EF, H), EF ** -0.5, 0.5)
    bias = noise(seeds[9], (H,), 0.5, 3.0, (), jnp.float32)
    w_out = noise(seeds[10], (H, W), (H * 64) ** -0.5, 0.03125)
    return {"node_feats": node_feats, "cotangent": cotangent, "edge_attr": edge_attr, "src_ids": src_ids, "dst_rel": dst_rel, "offsets": offsets, "counts": counts, "w_node": w_node, "w_edge": w_edge, "bias": bias, "w_out": w_out}


def reference(node_feats, cotangent, edge_attr, src_ids, dst_rel, offsets, counts, w_node, w_edge, bias, w_out):
    devs = N_SRC * N_DST
    per = BLK_DEV * BLOCK
    src_all = src_ids.reshape(devs, per)
    rel_all = dst_rel.reshape(devs, BLK_DEV, BLOCK)
    off_all = offsets.reshape(devs, BLK_DEV)
    cnt_all = counts.reshape(devs, BLK_DEV)
    attr_all = edge_attr.reshape(devs, per, EF)
    index_all = jnp.arange(devs, dtype=jnp.int32)

    def one(carry, items):
        agg, grads = carry
        src_k, rel_k, off_k, cnt_k, attr_k, k = items
        s_part = k // N_DST
        d_part = k % N_DST
        slots = lax.broadcasted_iota(jnp.int32, (BLK_DEV, BLOCK), 1)
        valid = (slots < cnt_k[:, None]).reshape(per)
        source = (d_part * (N_SRC * NODE_DEV) + src_k).astype(jnp.int32)
        target = (s_part * (N_DST * NODE_DEV) + off_k[:, None] + rel_k).reshape(per).astype(jnp.int32)
        x_e = node_feats[source]
        pre = jnp.dot(x_e, w_node, preferred_element_type=jnp.float32) + jnp.dot(attr_k, w_edge, preferred_element_type=jnp.float32) + bias
        hidden = jax.nn.silu(pre).astype(jnp.bfloat16)
        message = jnp.dot(hidden, w_out, preferred_element_type=jnp.float32)
        message = jnp.where(valid[:, None], message, jnp.float32(0.0))
        agg = agg.at[target].add(message)
        d_message = jnp.where(valid[:, None], cotangent[target], jnp.bfloat16(0.0)).astype(jnp.bfloat16)
        d_hidden = jnp.dot(d_message, w_out.T, preferred_element_type=jnp.float32)
        sig = jax.nn.sigmoid(pre)
        d_pre = (d_hidden * sig * (1.0 + pre * (1.0 - sig))).astype(jnp.bfloat16)
        d_attr = jnp.dot(d_pre, w_edge.T, preferred_element_type=jnp.float32).astype(jnp.bfloat16)
        d_source = jnp.dot(d_pre, w_node.T, preferred_element_type=jnp.float32)
        grads = grads.at[source].add(d_source)
        return (agg, grads), d_attr

    start = (jnp.zeros((NODES, W), jnp.float32), jnp.zeros((NODES, W), jnp.float32))
    (agg, grads), d_attrs = lax.scan(one, start, (src_all, rel_all, off_all, cnt_all, attr_all, index_all))
    return agg.astype(jnp.bfloat16), grads.astype(jnp.bfloat16), d_attrs.reshape(EDGES, EF)
```

```python
import math

import jax
import jax.numpy as jnp
from jax import lax
from jax.experimental import pallas as pl
from jax.experimental.pallas import tpu as pltpu
from jax.sharding import PartitionSpec as P

F32 = jnp.float32
BF16 = jnp.bfloat16
NN = (((1,), (0,)), ((), ()))
NT = (((1,), (1,)), ((), ()))
TN = (((0,), (0,)), ((), ()))
SMEM = pl.BlockSpec(memory_space=pltpu.SMEM)
VMEM = pl.BlockSpec(memory_space=pltpu.VMEM)
ANY = pl.BlockSpec(memory_space=pl.ANY)
CHUNK = 1536


def dot(a, b, dims=NN):
    return lax.dot_general(a, b, dims, preferred_element_type=F32)


def halves(x):
    high = x.astype(BF16)
    return high, (x - high.astype(F32)).astype(BF16)


def chunks(edges):
    return [pl.ds(c, min(CHUNK, edges - c)) for c in range(0, edges, CHUNK)]


def load(pairs, sems):
    copies = [pltpu.make_async_copy(*pair, sems.at[i]) for i, pair in enumerate(pairs)]
    for copy in copies:
        copy.start()
    return copies


def wait(copies):
    for copy in copies:
        copy.wait()


def edge_hots(off, cnt, rel, sid, dst_rows, src_rows):
    blocks, width = rel.shape
    lane = lax.broadcasted_iota(jnp.int32, (1, width), 1)
    dst_row = lax.broadcasted_iota(jnp.int32, (dst_rows, width), 0)
    src_row = lax.broadcasted_iota(jnp.int32, (src_rows, width), 0)
    for b in range(blocks):
        target = jnp.where(lane < cnt[b], rel[b : b + 1, :] + off[b], -1)
        to_dst = (dst_row == target).astype(F32)
        to_src = (src_row == sid[b : b + 1, :]).astype(F32)
        yield pl.ds(b * width, width), to_dst, to_src


def partner(me, n, k, back=False):
    if n & (n - 1) == 0:
        return me ^ k
    return lax.rem(me + (n - k if back else k), n)


def partner_of(me, n, k):
    return me ^ k if n & (n - 1) == 0 else (me + k) % n


def part(index, rows):
    return pl.ds(pl.multiple_of(index * rows, rows), rows)


INNER, NEAR = 4, 2
STEPS = (0, 2, 3, 1)


def place(index):
    return index // (NEAR * INNER), index // INNER % NEAR, index % INNER


def here():
    me = lax.axis_index("dst")
    return lax.div(me, NEAR * INNER), lax.rem(lax.div(me, INNER), NEAR), lax.rem(me, INNER)


def layer_steps(n_far):
    return [0, 1, *range(n_far * NEAR - 1, 1, -1)]


def layer_partner(far, near, n_far, k):
    return partner(far, n_far, k // NEAR) * NEAR + partner(near, NEAR, k % NEAR)


def swap(sends, to):
    pairs = [[(i, to(i, k)) for i in range(lax.axis_size("dst"))] for k in range(len(sends) + 1)]
    return [lax.ppermute(x, "dst", pairs[k + 1]) for k, x in enumerate(sends)]


def prepare(
    off_in, cnt_in, rel_in, sid_in, attr_in, cot_in, feat_in, bias_in, w_node_in, w_edge_in, w_out_in,
    rows_out, dst_out, src_out, cot_out, feat_out, bias_out, w_node_out, w_edge_out,
    w_out_out, off, cnt, rel, sid, sems,
):
    width = attr_in.shape[1]
    copies = load(
        [(off_in, off), (cnt_in, cnt), (rel_in, rel), (sid_in, sid)]
        + [(attr_in, rows_out.at[:, :width]), (cot_in, cot_out)]
        + [(feat_in, feat_out), (bias_in, bias_out)]
        + [(w_edge_in, w_edge_out), (w_node_in, w_node_out), (w_out_in, w_out_out)],
        sems,
    )
    wait(copies[:4])
    spare = rows_out.shape[1] - width - 2 * src_out.shape[0]
    fill = [jnp.zeros((spare, rel.shape[1]), F32)] if spare else []
    for at, to_dst, to_src in edge_hots(off, cnt, rel, sid, dst_out.shape[0], src_out.shape[0]):
        dst_out[:, at] = to_dst.astype(BF16)
        src_out[:, at] = to_src.astype(BF16)
        rows_out[at, width:] = jnp.concatenate([to_src, to_src, *fill], axis=0).T.astype(BF16)
    wait(copies[4:])


def forward(n_src, rows, dst_hot, bias, w_node, w_edge, w_out, *refs):
    feats, (half_out, sums_out, group, first, hidden) = refs[:n_src], refs[n_src:]
    me, owned = lax.axis_index("src"), feats[0].shape[0]
    for k, ref in enumerate(feats):
        group[part(lax.rem(me + k, n_src), owned), :] = ref[...]
    high, low = halves(0.5 * (dot(group[...], w_node[...]) + bias[...]))
    width, sources = w_edge.shape[0], group.shape[0]
    first[:width, :] = 0.5 * w_edge[...]
    first[width : width + sources, :] = high
    first[width + sources : width + 2 * sources, :] = low
    if first.shape[0] > width + 2 * sources:
        first[width + 2 * sources :, :] = jnp.zeros_like(first[width + 2 * sources :, :])
    for c in chunks(rows.shape[0]):
        half = dot(rows[c, :], first[...])
        half_out[c, :] = half
        hidden[c, :] = (half * jnp.tanh(half) + half).astype(BF16)
    high, low = halves(dot(dst_hot[...], hidden[...]))
    sums_out[...] = dot(high, w_out[...]) + dot(low, w_out[...])


def pack(n_far, owned, sums, *refs):
    parts, (cots_out, keep, *sends) = refs[:n_far], refs[n_far:]
    far, near, me = here()
    for k, ref in enumerate(parts):
        cots_out[part(partner(far, n_far, k, True), owned), :] = ref[...]
    rows = keep.shape[0]
    for k, out in enumerate([keep, *sends]):
        to = partner(me, INNER, STEPS[k])
        for z in range(n_far * NEAR):
            block = sums[part(z * INNER + to, owned), :]
            out[z * owned : (z + 1) * owned, :] = block.astype(out.dtype)
        if k:
            out[rows:, :] = cots_out[...]


def spread(n_far, owned, _, cots, keep, *refs):
    parts, (cots_out, own, *sends, total) = refs[: INNER - 1], refs[INNER - 1 :]
    far, near, me = here()
    rows = keep.shape[0]
    for k, ref in enumerate([cots] + [ref.at[rows:, :] for ref in parts]):
        owner = partner(me, INNER, STEPS[k], True)
        for f in range(n_far):
            block = ref[f * owned : (f + 1) * owned, :]
            cots_out[part(f * INNER + owner, owned), :] = block
    total[...] = sum((ref[:rows, :].astype(F32) for ref in parts), keep[...])
    for k, out in enumerate([own, *sends]):
        layer = layer_partner(far, near, n_far, layer_steps(n_far)[k])
        out[:owned, :] = total[part(layer, owned), :].astype(out.dtype)
    sends[0][owned:, :] = cots_out[...]


def slopes(_, half, dst_hot, slope_out, turned_out):
    for c in chunks(half.shape[0]):
        turned_out[c, :] = dst_hot[:, c].astype(F32).T.astype(BF16)
        t = jnp.tanh(half[c, :])
        slope_out[c, :] = 0.5 + 0.5 * (t + half[c, :] * (1.0 - t * t))


def backward(
    n_src, slope, dst_hot, src_hot, w_node, w_out, cots_near, came,
    d_pre, keep_out, send_out, total, cots,
):
    _, near, _ = here()
    owned, run = keep_out.shape[0], INNER * keep_out.shape[0]
    for f in range(cots_near.shape[0] // run):
        at = f * run
        cots[part(f * NEAR + near, run), :] = cots_near[at : at + run, :]
        at += owned
        cots[part(f * NEAR + 1 - near, run), :] = came[at : at + run, :]
    for c in chunks(slope.shape[0]):
        d_message = dot(dst_hot[c, :], cots[...]).astype(BF16)
        d_pre[c, :] = (dot(d_message, w_out[...], NT) * slope[c, :]).astype(BF16)
    high, low = halves(dot(src_hot[...], d_pre[...]))
    total[...] = dot(high, w_node[...], NT) + dot(low, w_node[...], NT)
    me = lax.axis_index("src")
    keep_out[...] = total[part(me, owned), :]
    for k in range(1, n_src):
        send_out[k - 1] = total[part(lax.rem(me + k, n_src), owned), :].astype(BF16)


def attributes(d_pre, w_edge, attr_out):
    for c in chunks(d_pre.shape[0]):
        attr_out[c, :] = dot(d_pre[c, :], w_edge[...], NT).astype(BF16)


def finish(n_agg, *refs):
    agg_out, grads_out = refs[-2:]
    owned = agg_out.shape[0]
    agg_out[...] = sum(ref[:owned, :].astype(F32) for ref in refs[:n_agg]).astype(BF16)
    grads_out[...] = sum(ref[...].astype(F32) for ref in refs[n_agg:-2]).astype(BF16)


def ahead(x, axis, k):
    n = lax.axis_size(axis)
    return lax.ppermute(x, axis, [((i + k) % n, i) for i in range(n)])


def local(
    node_feats, cotangent, edge_attr, src_ids, dst_rel, offsets, counts, w_node, w_edge, bias, w_out
):
    edges, attr_width = edge_attr.shape
    blocks = offsets.shape[0]
    width = edges // blocks
    owned, feat = node_feats.shape
    hidden = w_node.shape[1]
    n_src, n_dst = lax.axis_size("src"), lax.axis_size("dst")
    dst_rows, src_rows = owned * n_dst, owned * n_src
    n_far = n_dst // (NEAR * INNER)
    layers = n_far * NEAR
    params = pltpu.CompilerParams(vmem_limit_bytes=32 * 2**20)

    def array(*shape, dtype=BF16):
        return jax.ShapeDtypeStruct(shape, dtype)

    def rows_of(blocks, dtype=BF16):
        return array(blocks * owned, feat, dtype=dtype)

    def in_hbm(x):
        return pltpu.with_memory_space_constraint(x, pltpu.HBM)

    def call(kernel, name, args, outs, scratch=(), specs=None):
        return pl.pallas_call(
            kernel,
            name=name,
            in_specs=specs or [VMEM] * len(args),
            out_specs=[VMEM] * len(outs),
            out_shape=outs,
            scratch_shapes=list(scratch),
            compiler_params=params,
        )(*args)

    ints = [offsets, counts, dst_rel.reshape(blocks, width), src_ids.reshape(blocks, width)]
    bias = bias.reshape(1, hidden)
    feats = [ahead(node_feats, "src", k) for k in range(1, n_src)]
    depth = attr_width + 2 * src_rows
    depth += -depth % 128

    rows, dst_hot, src_hot, cots, own, *params_near = call(
        prepare,
        "prepare",
        [in_hbm(x) for x in (*ints, edge_attr, cotangent, node_feats, bias, w_node, w_edge, w_out)],
        [
            array(edges, depth),
            array(dst_rows, edges),
            array(src_rows, edges),
            rows_of(1),
            rows_of(1),
            array(*bias.shape, dtype=F32),
        ]
        + [array(*x.shape) for x in (w_node, w_edge, w_out)],
        [pltpu.SMEM(x.shape, jnp.int32) for x in ints[:2]]
        + [pltpu.VMEM(x.shape, jnp.int32) for x in ints[2:]]
        + [pltpu.SemaphoreType.DMA((11,))],
        [ANY] * 11,
    )
    _, w_node, w_edge, w_out = params_near

    def to_far(i, k):
        return i + (partner_of(place(i)[0], n_far, k) - place(i)[0]) * NEAR * INNER

    parts = swap([cotangent] * (n_far - 1), to_far)

    half, sums = call(
        lambda *refs: forward(n_src, *refs),
        "forward",
        [rows, dst_hot, *params_near, own, *feats],
        [array(edges, hidden, dtype=F32), rows_of(n_dst, F32)],
        [
            pltpu.VMEM((src_rows, feat), BF16),
            pltpu.VMEM((depth, hidden), BF16),
            pltpu.VMEM((edges, hidden), BF16),
        ],
    )

    cots, keep, *sends = call(
        lambda *refs: pack(n_far, owned, *refs),
        "pack",
        [sums, cots, *parts],
        [rows_of(n_far), rows_of(layers, F32)] + [rows_of(layers + n_far)] * (INNER - 1),
    )
    parts = swap(sends, lambda i, k: i - i % INNER + partner_of(i % INNER, INNER, STEPS[k]))

    slope, turned = call(
        slopes,
        "slopes",
        [keep, half, dst_hot],
        [array(edges, hidden, dtype=F32), array(edges, dst_rows)],
    )

    beside = n_far * INNER
    cots, keep, *sends = call(
        lambda *refs: spread(n_far, owned, *refs),
        "spread",
        [slope, cots, keep, *parts],
        [rows_of(beside), rows_of(1, F32), rows_of(1 + beside)] + [rows_of(1, F32)] * (layers - 2),
        [pltpu.VMEM((layers * owned, feat), F32)],
        [ANY] + [VMEM] * (1 + INNER),
    )

    def to_layer(i, k):
        far, near, me = place(i)
        k = layer_steps(n_far)[k]
        to = partner_of(far, n_far, k // NEAR) * NEAR + partner_of(near, NEAR, k % NEAR)
        return to * INNER + me

    parts = swap(sends, to_layer)

    d_pre, keep_grads, send_grads = call(
        lambda *refs: backward(n_src, *refs),
        "backward",
        [slope, turned, src_hot, w_node, w_out, cots, parts[0]],
        [array(edges, hidden), rows_of(1, F32), array(n_src - 1, owned, feat)],
        [pltpu.VMEM((src_rows, feat), F32), pltpu.VMEM((dst_rows, feat), BF16)],
    )

    others = [ahead(send_grads[k - 1], "src", n_src - k) for k in range(1, n_src)]

    (attr_grads,) = call(
        attributes,
        "attributes",
        [d_pre, w_edge],
        [array(edges, attr_width)],
    )

    aggregated, node_grads = call(
        lambda *refs: finish(1 + len(parts), *refs),
        "finish",
        [keep, *parts, keep_grads, *others],
        [rows_of(1), rows_of(1)],
    )
    return aggregated, node_grads, attr_grads


def solution(mesh):
    in_specs = (
        P(("dst", "src"), None),
        P(("src", "dst"), None),
        P(("src", "dst"), None),
        P(("src", "dst")),
        P(("src", "dst")),
        P(("src", "dst")),
        P(("src", "dst")),
        P(),
        P(),
        P(),
        P(),
    )
    out_specs = (P(("src", "dst"), None), P(("dst", "src"), None), P(("src", "dst"), None))
    return jax.shard_map(local, mesh=mesh, in_specs=in_specs, out_specs=out_specs, check_vma=False)
```

```python
import math

import jax
import jax.numpy as jnp
from jax import lax
from jax.experimental import pallas as pl
from jax.experimental.pallas import tpu as pltpu
from jax.sharding import PartitionSpec as P

F32 = jnp.float32
BF16 = jnp.bfloat16
NN = (((1,), (0,)), ((), ()))
NT = (((1,), (1,)), ((), ()))
TN = (((0,), (0,)), ((), ()))
SMEM = pl.BlockSpec(memory_space=pltpu.SMEM)
VMEM = pl.BlockSpec(memory_space=pltpu.VMEM)
ANY = pl.BlockSpec(memory_space=pl.ANY)
CHUNK = 1536
PARTS = 3


def dot(a, b, dims=NN):
    return lax.dot_general(a, b, dims, preferred_element_type=F32)


def halves(x):
    high = x.astype(BF16)
    return high, (x - high.astype(F32)).astype(BF16)


def chunks(edges):
    return [pl.ds(c, min(CHUNK, edges - c)) for c in range(0, edges, CHUNK)]


def load(pairs, sems):
    copies = [pltpu.make_async_copy(*pair, sems.at[i]) for i, pair in enumerate(pairs)]
    for copy in copies:
        copy.start()
    return copies


def wait(copies):
    for copy in copies:
        copy.wait()


def edge_hots(off, cnt, rel, sid, dst_rows, src_rows):
    blocks, width = rel.shape
    lane = lax.broadcasted_iota(jnp.int32, (1, width), 1)
    dst_row = lax.broadcasted_iota(jnp.int32, (dst_rows, width), 0)
    src_row = lax.broadcasted_iota(jnp.int32, (src_rows, width), 0)
    for b in range(blocks):
        target = jnp.where(lane < cnt[b], rel[b : b + 1, :] + off[b], -1)
        to_dst = (dst_row == target).astype(F32)
        to_src = (src_row == sid[b : b + 1, :]).astype(F32)
        yield pl.ds(b * width, width), to_dst, to_src


def partner(me, n, k, back=False):
    if n & (n - 1) == 0:
        return me ^ k
    return lax.rem(me + (n - k if back else k), n)


def partner_of(me, n, k):
    return me ^ k if n & (n - 1) == 0 else (me + k) % n


def part(index, rows):
    return pl.ds(pl.multiple_of(index * rows, rows), rows)


INNER, NEAR = 4, 2
STEPS = (0, 2, 3, 1)


def block(far, near, me):
    return far * (NEAR * INNER) + (me >> 1) * 4 + near * 2 + (me & 1)


def place(index):
    return index // (NEAR * INNER), (index >> 1) & 1, ((index >> 2) & 1) * 2 + (index & 1)


def here():
    me = lax.axis_index("dst")
    return lax.div(me, NEAR * INNER), (me >> 1) & 1, ((me >> 2) & 1) * 2 + (me & 1)


def layer_partner(far, near, n_far, k):
    return partner(far, n_far, k // NEAR) * NEAR + partner(near, NEAR, k % NEAR)


def swap(sends, to):
    pairs = [[(i, to(i, k)) for i in range(lax.axis_size("dst"))] for k in range(len(sends) + 1)]
    return [lax.ppermute(x, "dst", pairs[k + 1]) for k, x in enumerate(sends)]


def prepare(
    off_in, cnt_in, rel_in, sid_in, attr_in, cot_in, feat_in, bias_in, w_node_in, w_edge_in, w_out_in,
    rows_out, dst_out, turned_out, src_out, cot_out, feat_out, bias_out, w_node_out, w_edge_out,
    w_out_out, off, cnt, rel, sid, sems,
):
    width = attr_in.shape[1]
    copies = load(
        [(off_in, off), (cnt_in, cnt), (rel_in, rel), (sid_in, sid)]
        + [(attr_in, rows_out.at[:, :width]), (cot_in, cot_out)]
        + [(feat_in, feat_out), (bias_in, bias_out)]
        + [(w_edge_in, w_edge_out), (w_node_in, w_node_out), (w_out_in, w_out_out)],
        sems,
    )
    wait(copies[:4])
    spare = rows_out.shape[1] - width - PARTS * src_out.shape[0]
    fill = [jnp.zeros((spare, rel.shape[1]), F32)] if spare else []
    for at, to_dst, to_src in edge_hots(off, cnt, rel, sid, dst_out.shape[0], src_out.shape[0]):
        dst_out[:, at] = to_dst.astype(BF16)
        turned_out[at, :] = to_dst.T.astype(BF16)
        src_out[:, at] = to_src.astype(BF16)
        rows_out[at, width:] = jnp.concatenate([to_src] * PARTS + fill, axis=0).T.astype(BF16)
    wait(copies[4:])


def forward(n_src, rows, dst_hot, bias, w_node, w_edge, w_out, *refs):
    feats, (half_out, sums_out, group, first, hidden) = refs[:n_src], refs[n_src:]
    me, owned = lax.axis_index("src"), feats[0].shape[0]
    for k, ref in enumerate(feats):
        group[part(lax.rem(me + k, n_src), owned), :] = ref[...]
    table = 0.5 * (dot(group[...], w_node[...]) + bias[...])
    first[: w_edge.shape[0], :] = 0.5 * w_edge[...]
    end = w_edge.shape[0]
    for _ in range(PARTS):
        piece = table.astype(BF16)
        first[end : end + group.shape[0], :] = piece
        table = table - piece.astype(F32)
        end += group.shape[0]
    if first.shape[0] > end:
        first[end:, :] = jnp.zeros_like(first[end:, :])
    for c in chunks(rows.shape[0]):
        half = dot(rows[c, :], first[...])
        half_out[c, :] = half
        hidden[c, :] = (half * jnp.tanh(half) + half).astype(BF16)
    high, low = halves(dot(dst_hot[...], hidden[...]))
    sums_out[...] = dot(high, w_out[...]) + dot(low, w_out[...])


def pack(n_far, owned, sums, *refs):
    parts, (cots_out, keep, *sends) = refs[:n_far], refs[n_far:]
    far, near, me = here()
    for k, ref in enumerate(parts):
        cots_out[part(partner(far, n_far, k, True), owned), :] = ref[...]
    rows = keep.shape[0]
    for k, out in enumerate([keep, *sends]):
        to = partner(me, INNER, STEPS[k])
        for z in range(n_far * NEAR):
            whose = jnp.where(z // NEAR == far, to, to ^ 1)
            its = sums[part(block(z // NEAR, z % NEAR, whose), owned), :]
            out[z * owned : (z + 1) * owned, :] = its.astype(out.dtype)
        if k:
            out[rows:, :] = cots_out[...]


def spread(n_far, owned, _, cots, keep, *refs):
    parts, (cots_out, own, *sends, total) = refs[: INNER - 1], refs[INNER - 1 :]
    far, near, me = here()
    rows = keep.shape[0]
    for k, ref in enumerate([cots] + [ref.at[rows:, :] for ref in parts]):
        owner = partner(me, INNER, STEPS[k], True)
        for f in range(n_far):
            whose = jnp.where(f == far, owner, owner ^ 1)
            cots_out[part(f * INNER + whose, owned), :] = ref[f * owned : (f + 1) * owned, :]
    total[...] = sum((ref[:rows, :].astype(F32) for ref in parts), keep[...])
    for k, out in enumerate([own, *sends]):
        layer = layer_partner(far, near, n_far, k)
        out[:owned, :] = total[part(layer, owned), :].astype(out.dtype)
    sends[0][owned:, :] = cots_out[...]


def slopes(_, half, w_node, w_out, slope_out, w_node_out, w_out_out):
    w_out_out[...] = w_out[...].T
    w_node_out[...] = w_node[...].T
    for c in chunks(half.shape[0]):
        t = jnp.tanh(half[c, :])
        slope_out[c, :] = 0.5 + 0.5 * (t + half[c, :] * (1.0 - t * t))


def backward(
    n_src, slope, dst_hot, src_hot, w_node, w_out, cots_near, came,
    d_pre, keep_out, send_out, total, cots,
):
    _, near, _ = here()
    owned, run = keep_out.shape[0], 2 * keep_out.shape[0]
    for pair in range(cots_near.shape[0] // run):
        at = pair * run
        cots[part(pair * NEAR + near, run), :] = cots_near[at : at + run, :]
        at += owned
        cots[part(pair * NEAR + 1 - near, run), :] = came[at : at + run, :]
    for c in chunks(slope.shape[0]):
        d_message = dot(dst_hot[c, :], cots[...]).astype(BF16)
        d_pre[c, :] = (dot(d_message, w_out[...]) * slope[c, :]).astype(BF16)
    high, low = halves(dot(src_hot[...], d_pre[...]))
    total[...] = dot(high, w_node[...]) + dot(low, w_node[...])
    me = lax.axis_index("src")
    keep_out[...] = total[part(me, owned), :]
    for k in range(1, n_src):
        send_out[k - 1] = total[part(lax.rem(me + k, n_src), owned), :].astype(BF16)


def attributes(d_pre, w_edge, attr_out):
    for c in chunks(d_pre.shape[0]):
        attr_out[c, :] = dot(d_pre[c, :], w_edge[...], NT).astype(BF16)


def finish(n_agg, *refs):
    agg_out, grads_out = refs[-2:]
    owned = agg_out.shape[0]
    agg_out[...] = sum(ref[:owned, :].astype(F32) for ref in refs[:n_agg]).astype(BF16)
    grads_out[...] = sum(ref[...].astype(F32) for ref in refs[n_agg:-2]).astype(BF16)


def ahead(x, axis, k):
    n = lax.axis_size(axis)
    return lax.ppermute(x, axis, [((i + k) % n, i) for i in range(n)])


def local(
    node_feats, cotangent, edge_attr, src_ids, dst_rel, offsets, counts, w_node, w_edge, bias, w_out
):
    edges, attr_width = edge_attr.shape
    blocks = offsets.shape[0]
    width = edges // blocks
    owned, feat = node_feats.shape
    hidden = w_node.shape[1]
    n_src, n_dst = lax.axis_size("src"), lax.axis_size("dst")
    dst_rows, src_rows = owned * n_dst, owned * n_src
    n_far = n_dst // (NEAR * INNER)
    layers = n_far * NEAR
    params = pltpu.CompilerParams(vmem_limit_bytes=32 * 2**20)

    def array(*shape, dtype=BF16):
        return jax.ShapeDtypeStruct(shape, dtype)

    def rows_of(blocks, dtype=BF16):
        return array(blocks * owned, feat, dtype=dtype)

    def in_hbm(x):
        return pltpu.with_memory_space_constraint(x, pltpu.HBM)

    def call(kernel, name, args, outs, scratch=(), specs=None):
        return pl.pallas_call(
            kernel,
            name=name,
            in_specs=specs or [VMEM] * len(args),
            out_specs=[VMEM] * len(outs),
            out_shape=outs,
            scratch_shapes=list(scratch),
            compiler_params=params,
        )(*args)

    ints = [offsets, counts, dst_rel.reshape(blocks, width), src_ids.reshape(blocks, width)]
    bias = bias.reshape(1, hidden)
    feats = [ahead(node_feats, "src", k) for k in range(1, n_src)]
    depth = attr_width + PARTS * src_rows
    depth += -depth % 128

    rows, dst_hot, turned, src_hot, cots, own, *params_near = call(
        prepare,
        "prepare",
        [in_hbm(x) for x in (*ints, edge_attr, cotangent, node_feats, bias, w_node, w_edge, w_out)],
        [
            array(edges, depth),
            array(dst_rows, edges),
            array(edges, dst_rows),
            array(src_rows, edges),
            rows_of(1),
            rows_of(1),
            array(*bias.shape, dtype=F32),
        ]
        + [array(*x.shape) for x in (w_node, w_edge, w_out)],
        [pltpu.SMEM(x.shape, jnp.int32) for x in ints[:2]]
        + [pltpu.VMEM(x.shape, jnp.int32) for x in ints[2:]]
        + [pltpu.SemaphoreType.DMA((11,))],
        [ANY] * 11,
    )
    _, w_node, w_edge, w_out = params_near

    def to_far(i, k):
        far, near, me = place(i)
        return block(partner_of(far, n_far, k), near, me ^ 1)

    parts = swap([cotangent] * (n_far - 1), to_far)

    half, sums = call(
        lambda *refs: forward(n_src, *refs),
        "forward",
        [rows, dst_hot, *params_near, own, *feats],
        [array(edges, hidden, dtype=F32), rows_of(n_dst, F32)],
        [
            pltpu.VMEM((src_rows, feat), BF16),
            pltpu.VMEM((depth, hidden), BF16),
            pltpu.VMEM((edges, hidden), BF16),
        ],
    )

    cots, keep, *sends = call(
        lambda *refs: pack(n_far, owned, *refs),
        "pack",
        [sums, cots, *parts],
        [rows_of(n_far), rows_of(layers, F32)] + [rows_of(layers + n_far)] * (INNER - 1),
    )
    def to_inner(i, k):
        far, near, me = place(i)
        return block(far, near, partner_of(me, INNER, STEPS[k]))

    parts = swap(sends, to_inner)

    slope, w_node, w_out = call(
        slopes,
        "slopes",
        [keep, half, w_node, w_out],
        [array(edges, hidden, dtype=F32)] + [array(*x.shape[::-1]) for x in (w_node, w_out)],
    )

    beside = n_far * INNER
    cots, keep, *sends = call(
        lambda *refs: spread(n_far, owned, *refs),
        "spread",
        [slope, cots, keep, *parts],
        [rows_of(beside), rows_of(1, F32), rows_of(1 + beside)] + [rows_of(1, F32)] * (layers - 2),
        [pltpu.VMEM((layers * owned, feat), F32)],
        [ANY] + [VMEM] * (1 + INNER),
    )

    def to_layer(i, k):
        far, near, me = place(i)
        far, near = partner_of(far, n_far, k // NEAR), partner_of(near, NEAR, k % NEAR)
        return block(far, near, me ^ (k >= NEAR))

    parts = swap(sends, to_layer)

    d_pre, keep_grads, send_grads = call(
        lambda *refs: backward(n_src, *refs),
        "backward",
        [slope, turned, src_hot, w_node, w_out, cots, parts[0]],
        [array(edges, hidden), rows_of(1, F32), array(n_src - 1, owned, feat)],
        [pltpu.VMEM((src_rows, feat), F32), pltpu.VMEM((dst_rows, feat), BF16)],
    )

    others = [ahead(send_grads[k - 1], "src", n_src - k) for k in range(1, n_src)]

    (attr_grads,) = call(
        attributes,
        "attributes",
        [d_pre, w_edge],
        [array(edges, attr_width)],
    )

    aggregated, node_grads = call(
        lambda *refs: finish(1 + len(parts), *refs),
        "finish",
        [keep, *parts, keep_grads, *others],
        [rows_of(1), rows_of(1)],
    )
    return aggregated, node_grads, attr_grads


def solution(mesh):
    in_specs = (
        P(("dst", "src"), None),
        P(("src", "dst"), None),
        P(("src", "dst"), None),
        P(("src", "dst")),
        P(("src", "dst")),
        P(("src", "dst")),
        P(("src", "dst")),
        P(),
        P(),
        P(),
        P(),
    )
    out_specs = (P(("src", "dst"), None), P(("dst", "src"), None), P(("src", "dst"), None))
    return jax.shard_map(local, mesh=mesh, in_specs=in_specs, out_specs=out_specs, check_vma=False)
```

```python
import math

import jax
import jax.numpy as jnp
from jax import lax
from jax.experimental import pallas as pl
from jax.experimental.pallas import tpu as pltpu
from jax.sharding import PartitionSpec as P

F32 = jnp.float32
BF16 = jnp.bfloat16
NN = (((1,), (0,)), ((), ()))
NT = (((1,), (1,)), ((), ()))
TN = (((0,), (0,)), ((), ()))
SMEM = pl.BlockSpec(memory_space=pltpu.SMEM)
VMEM = pl.BlockSpec(memory_space=pltpu.VMEM)
ANY = pl.BlockSpec(memory_space=pl.ANY)
CHUNK = 1536
PARTS = 3


def dot(a, b, dims=NN):
    return lax.dot_general(a, b, dims, preferred_element_type=F32)


def halves(x):
    high = x.astype(BF16)
    return high, (x - high.astype(F32)).astype(BF16)


def chunks(edges):
    return [pl.ds(c, min(CHUNK, edges - c)) for c in range(0, edges, CHUNK)]


def load(pairs, sems):
    copies = [pltpu.make_async_copy(*pair, sems.at[i]) for i, pair in enumerate(pairs)]
    for copy in copies:
        copy.start()
    return copies


def wait(copies):
    for copy in copies:
        copy.wait()


def edge_hots(off, cnt, rel, sid, dst_rows, src_rows):
    blocks, width = rel.shape
    lane = lax.broadcasted_iota(jnp.int32, (1, width), 1)
    dst_row = lax.broadcasted_iota(jnp.int32, (dst_rows, width), 0)
    src_row = lax.broadcasted_iota(jnp.int32, (src_rows, width), 0)
    for b in range(blocks):
        target = jnp.where(lane < cnt[b], rel[b : b + 1, :] + off[b], -1)
        to_dst = (dst_row == target).astype(F32)
        to_src = (src_row == sid[b : b + 1, :]).astype(F32)
        yield pl.ds(b * width, width), to_dst, to_src


def partner(me, n, k, back=False):
    if n & (n - 1) == 0:
        return me ^ k
    return lax.rem(me + (n - k if back else k), n)


def partner_of(me, n, k):
    return me ^ k if n & (n - 1) == 0 else (me + k) % n


def part(index, rows):
    return pl.ds(pl.multiple_of(index * rows, rows), rows)


INNER, NEAR = 4, 2
STEPS = (0, 2, 3, 1)


def block(far, near, me):
    return far * (NEAR * INNER) + (me >> 1) * 4 + near * 2 + (me & 1)


def place(index):
    return index // (NEAR * INNER), (index >> 1) & 1, ((index >> 2) & 1) * 2 + (index & 1)


def here():
    me = lax.axis_index("dst")
    return lax.div(me, NEAR * INNER), (me >> 1) & 1, ((me >> 2) & 1) * 2 + (me & 1)


def layer_partner(far, near, n_far, k):
    return partner(far, n_far, k // NEAR) * NEAR + partner(near, NEAR, k % NEAR)


def swap(sends, to):
    pairs = [[(i, to(i, k)) for i in range(lax.axis_size("dst"))] for k in range(len(sends) + 1)]
    return [lax.ppermute(x, "dst", pairs[k + 1]) for k, x in enumerate(sends)]


def prepare(
    off_in, cnt_in, rel_in, sid_in, attr_in, cot_in, feat_in, bias_in, w_node_in, w_edge_in, w_out_in,
    rows_out, dst_out, turned_out, src_out, cot_out, feat_out, bias_out, w_node_out, w_edge_out,
    w_out_out, off, cnt, rel, sid, sems,
):
    width = attr_in.shape[1]
    copies = load(
        [(off_in, off), (cnt_in, cnt), (rel_in, rel), (sid_in, sid)]
        + [(attr_in, rows_out.at[:, :width]), (cot_in, cot_out)]
        + [(feat_in, feat_out), (bias_in, bias_out)]
        + [(w_edge_in, w_edge_out), (w_node_in, w_node_out), (w_out_in, w_out_out)],
        sems,
    )
    wait(copies[:4])
    spare = rows_out.shape[1] - width - PARTS * src_out.shape[0]
    fill = [jnp.zeros((spare, rel.shape[1]), F32)] if spare else []
    for at, to_dst, to_src in edge_hots(off, cnt, rel, sid, dst_out.shape[0], src_out.shape[0]):
        dst_out[:, at] = to_dst.astype(BF16)
        turned_out[at, :] = to_dst.T.astype(BF16)
        src_out[:, at] = to_src.astype(BF16)
        rows_out[at, width:] = jnp.concatenate([to_src] * PARTS + fill, axis=0).T.astype(BF16)
    wait(copies[4:])


def forward(n_src, rows, dst_hot, bias, w_node, w_edge, w_out, *refs):
    feats, (half_out, sums_out, group, first, hidden) = refs[:n_src], refs[n_src:]
    me, owned = lax.axis_index("src"), feats[0].shape[0]
    for k, ref in enumerate(feats):
        group[part(lax.rem(me + k, n_src), owned), :] = ref[...]
    table = 0.5 * (dot(group[...], w_node[...]) + bias[...])
    first[: w_edge.shape[0], :] = 0.5 * w_edge[...]
    end = w_edge.shape[0]
    for _ in range(PARTS):
        piece = table.astype(BF16)
        first[end : end + group.shape[0], :] = piece
        table = table - piece.astype(F32)
        end += group.shape[0]
    if first.shape[0] > end:
        first[end:, :] = jnp.zeros_like(first[end:, :])
    for c in chunks(rows.shape[0]):
        half = dot(rows[c, :], first[...])
        half_out[c, :] = half
        hidden[c, :] = (half * jnp.tanh(half) + half).astype(BF16)
    high, low = halves(dot(dst_hot[...], hidden[...]))
    sums_out[...] = dot(high, w_out[...]) + dot(low, w_out[...])


def pack(n_far, owned, sums, *refs):
    parts, (cots_out, keep, *sends) = refs[:n_far], refs[n_far:]
    far, near, me = here()
    for k, ref in enumerate(parts):
        cots_out[part(partner(far, n_far, k, True), owned), :] = ref[...]
    rows = keep.shape[0]
    for k, out in enumerate([keep, *sends]):
        to = partner(me, INNER, STEPS[k])
        for z in range(n_far * NEAR):
            whose = jnp.where(z == far * NEAR + near, to, to ^ 1)
            its = sums[part(block(z // NEAR, z % NEAR, whose), owned), :]
            out[z * owned : (z + 1) * owned, :] = its.astype(out.dtype)
        if k:
            out[rows:, :] = cots_out[...]


def spread(n_far, owned, _, cots, keep, *refs):
    parts, (cots_out, own, *sends, total) = refs[: INNER - 1], refs[INNER - 1 :]
    far, near, me = here()
    rows = keep.shape[0]
    for k, ref in enumerate([cots] + [ref.at[rows:, :] for ref in parts]):
        owner = partner(me, INNER, STEPS[k], True)
        for f in range(n_far):
            whose = jnp.where(f == far, owner, owner ^ 1)
            cots_out[part(f * INNER + whose, owned), :] = ref[f * owned : (f + 1) * owned, :]
    total[...] = sum((ref[:rows, :].astype(F32) for ref in parts), keep[...])
    for k, out in enumerate([own, *sends]):
        layer = layer_partner(far, near, n_far, k)
        out[:owned, :] = total[part(layer, owned), :].astype(out.dtype)
    sends[0][owned:, :] = cots_out[...]


def slopes(_, half, w_node, w_out, slope_out, w_node_out, w_out_out):
    w_out_out[...] = w_out[...].T
    w_node_out[...] = w_node[...].T
    for c in chunks(half.shape[0]):
        t = jnp.tanh(half[c, :])
        slope_out[c, :] = 0.5 + 0.5 * (t + half[c, :] * (1.0 - t * t))


def backward(
    n_src, slope, dst_hot, src_hot, w_node, w_out, cots_near, came,
    d_pre, keep_out, send_out, total, cots,
):
    _, near, _ = here()
    owned, run = keep_out.shape[0], 2 * keep_out.shape[0]
    for pair in range(cots_near.shape[0] // run):
        at = pair * run
        cots[part(pair * NEAR + near, run), :] = cots_near[at : at + run, :]
        at += owned
        cots[part(pair * NEAR + 1 - near, run), :] = came[at : at + run, :]
    for c in chunks(slope.shape[0]):
        d_message = dot(dst_hot[c, :], cots[...]).astype(BF16)
        d_pre[c, :] = (dot(d_message, w_out[...]) * slope[c, :]).astype(BF16)
    high, low = halves(dot(src_hot[...], d_pre[...]))
    total[...] = dot(high, w_node[...]) + dot(low, w_node[...])
    me = lax.axis_index("src")
    keep_out[...] = total[part(me, owned), :]
    for k in range(1, n_src):
        send_out[k - 1] = total[part(lax.rem(me + k, n_src), owned), :].astype(BF16)


def attributes(d_pre, w_edge, attr_out):
    for c in chunks(d_pre.shape[0]):
        attr_out[c, :] = dot(d_pre[c, :], w_edge[...], NT).astype(BF16)


def finish(n_agg, *refs):
    agg_out, grads_out = refs[-2:]
    owned = agg_out.shape[0]
    agg_out[...] = sum(ref[:owned, :].astype(F32) for ref in refs[:n_agg]).astype(BF16)
    grads_out[...] = sum(ref[...].astype(F32) for ref in refs[n_agg:-2]).astype(BF16)


def ahead(x, axis, k):
    n = lax.axis_size(axis)
    return lax.ppermute(x, axis, [((i + k) % n, i) for i in range(n)])


def local(
    node_feats, cotangent, edge_attr, src_ids, dst_rel, offsets, counts, w_node, w_edge, bias, w_out
):
    edges, attr_width = edge_attr.shape
    blocks = offsets.shape[0]
    width = edges // blocks
    owned, feat = node_feats.shape
    hidden = w_node.shape[1]
    n_src, n_dst = lax.axis_size("src"), lax.axis_size("dst")
    dst_rows, src_rows = owned * n_dst, owned * n_src
    n_far = n_dst // (NEAR * INNER)
    layers = n_far * NEAR
    params = pltpu.CompilerParams(vmem_limit_bytes=32 * 2**20)

    def array(*shape, dtype=BF16):
        return jax.ShapeDtypeStruct(shape, dtype)

    def rows_of(blocks, dtype=BF16):
        return array(blocks * owned, feat, dtype=dtype)

    def in_hbm(x):
        return pltpu.with_memory_space_constraint(x, pltpu.HBM)

    def call(kernel, name, args, outs, scratch=(), specs=None):
        return pl.pallas_call(
            kernel,
            name=name,
            in_specs=specs or [VMEM] * len(args),
            out_specs=[VMEM] * len(outs),
            out_shape=outs,
            scratch_shapes=list(scratch),
            compiler_params=params,
        )(*args)

    ints = [offsets, counts, dst_rel.reshape(blocks, width), src_ids.reshape(blocks, width)]
    bias = bias.reshape(1, hidden)
    feats = [ahead(node_feats, "src", k) for k in range(1, n_src)]
    depth = attr_width + PARTS * src_rows
    depth += -depth % 128

    rows, dst_hot, turned, src_hot, cots, own, *params_near = call(
        prepare,
        "prepare",
        [in_hbm(x) for x in (*ints, edge_attr, cotangent, node_feats, bias, w_node, w_edge, w_out)],
        [
            array(edges, depth),
            array(dst_rows, edges),
            array(edges, dst_rows),
            array(src_rows, edges),
            rows_of(1),
            rows_of(1),
            array(*bias.shape, dtype=F32),
        ]
        + [array(*x.shape) for x in (w_node, w_edge, w_out)],
        [pltpu.SMEM(x.shape, jnp.int32) for x in ints[:2]]
        + [pltpu.VMEM(x.shape, jnp.int32) for x in ints[2:]]
        + [pltpu.SemaphoreType.DMA((11,))],
        [ANY] * 11,
    )
    _, w_node, w_edge, w_out = params_near

    def to_far(i, k):
        far, near, me = place(i)
        return block(partner_of(far, n_far, k), near, me ^ 1)

    parts = swap([cotangent] * (n_far - 1), to_far)

    half, sums = call(
        lambda *refs: forward(n_src, *refs),
        "forward",
        [rows, dst_hot, *params_near, own, *feats],
        [array(edges, hidden, dtype=F32), rows_of(n_dst, F32)],
        [
            pltpu.VMEM((src_rows, feat), BF16),
            pltpu.VMEM((depth, hidden), BF16),
            pltpu.VMEM((edges, hidden), BF16),
        ],
    )

    cots, keep, *sends = call(
        lambda *refs: pack(n_far, owned, *refs),
        "pack",
        [sums, cots, *parts],
        [rows_of(n_far), rows_of(layers, F32)] + [rows_of(layers + n_far)] * (INNER - 1),
    )
    def to_inner(i, k):
        far, near, me = place(i)
        return block(far, near, partner_of(me, INNER, STEPS[k]))

    parts = swap(sends, to_inner)

    slope, w_node, w_out = call(
        slopes,
        "slopes",
        [keep, half, w_node, w_out],
        [array(edges, hidden, dtype=F32)] + [array(*x.shape[::-1]) for x in (w_node, w_out)],
    )

    beside = n_far * INNER
    cots, keep, *sends = call(
        lambda *refs: spread(n_far, owned, *refs),
        "spread",
        [slope, cots, keep, *parts],
        [rows_of(beside), rows_of(1, F32), rows_of(1 + beside)] + [rows_of(1, F32)] * (layers - 2),
        [pltpu.VMEM((layers * owned, feat), F32)],
        [ANY] + [VMEM] * (1 + INNER),
    )

    def to_layer(i, k):
        far, near, me = place(i)
        far, near = partner_of(far, n_far, k // NEAR), partner_of(near, NEAR, k % NEAR)
        return block(far, near, me ^ 1)

    parts = swap(sends, to_layer)

    d_pre, keep_grads, send_grads = call(
        lambda *refs: backward(n_src, *refs),
        "backward",
        [slope, turned, src_hot, w_node, w_out, cots, parts[0]],
        [array(edges, hidden), rows_of(1, F32), array(n_src - 1, owned, feat)],
        [pltpu.VMEM((src_rows, feat), F32), pltpu.VMEM((dst_rows, feat), BF16)],
    )

    others = [ahead(send_grads[k - 1], "src", n_src - k) for k in range(1, n_src)]

    (attr_grads,) = call(
        attributes,
        "attributes",
        [d_pre, w_edge],
        [array(edges, attr_width)],
    )

    aggregated, node_grads = call(
        lambda *refs: finish(1 + len(parts), *refs),
        "finish",
        [keep, *parts, keep_grads, *others],
        [rows_of(1), rows_of(1)],
    )
    return aggregated, node_grads, attr_grads


def solution(mesh):
    in_specs = (
        P(("dst", "src"), None),
        P(("src", "dst"), None),
        P(("src", "dst"), None),
        P(("src", "dst")),
        P(("src", "dst")),
        P(("src", "dst")),
        P(("src", "dst")),
        P(),
        P(),
        P(),
        P(),
    )
    out_specs = (P(("src", "dst"), None), P(("dst", "src"), None), P(("src", "dst"), None))
    return jax.shard_map(local, mesh=mesh, in_specs=in_specs, out_specs=out_specs, check_vma=False)
```

```python
import math

import jax
import jax.numpy as jnp
from jax import lax
from jax.experimental import pallas as pl
from jax.experimental.pallas import tpu as pltpu
from jax.sharding import PartitionSpec as P

F32 = jnp.float32
BF16 = jnp.bfloat16
NN = (((1,), (0,)), ((), ()))
NT = (((1,), (1,)), ((), ()))
TN = (((0,), (0,)), ((), ()))
SMEM = pl.BlockSpec(memory_space=pltpu.SMEM)
VMEM = pl.BlockSpec(memory_space=pltpu.VMEM)
ANY = pl.BlockSpec(memory_space=pl.ANY)
CHUNK = 1536
PARTS = 3


def dot(a, b, dims=NN):
    return lax.dot_general(a, b, dims, preferred_element_type=F32)


def halves(x):
    high = x.astype(BF16)
    return high, (x - high.astype(F32)).astype(BF16)


def chunks(edges):
    return [pl.ds(c, min(CHUNK, edges - c)) for c in range(0, edges, CHUNK)]


def load(pairs, sems):
    copies = [pltpu.make_async_copy(*pair, sems.at[i]) for i, pair in enumerate(pairs)]
    for copy in copies:
        copy.start()
    return copies


def wait(copies):
    for copy in copies:
        copy.wait()


def edge_hots(off, cnt, rel, sid, dst_rows, src_rows):
    blocks, width = rel.shape
    lane = lax.broadcasted_iota(jnp.int32, (1, width), 1)
    dst_row = lax.broadcasted_iota(jnp.int32, (dst_rows, width), 0)
    src_row = lax.broadcasted_iota(jnp.int32, (src_rows, width), 0)
    for b in range(blocks):
        target = jnp.where(lane < cnt[b], rel[b : b + 1, :] + off[b], -1)
        to_dst = (dst_row == target).astype(F32)
        to_src = (src_row == sid[b : b + 1, :]).astype(F32)
        yield pl.ds(b * width, width), to_dst, to_src


def partner(me, n, k, back=False):
    if n & (n - 1) == 0:
        return me ^ k
    return lax.rem(me + (n - k if back else k), n)


def partner_of(me, n, k):
    return me ^ k if n & (n - 1) == 0 else (me + k) % n


def part(index, rows):
    return pl.ds(pl.multiple_of(index * rows, rows), rows)


INNER, NEAR = 4, 2
STEPS = (0, 2, 3, 1)


def block(far, near, me):
    return far * (NEAR * INNER) + (me >> 1) * 4 + near * 2 + (me & 1)


def place(index):
    return index // (NEAR * INNER), (index >> 1) & 1, ((index >> 2) & 1) * 2 + (index & 1)


def here():
    me = lax.axis_index("dst")
    return lax.div(me, NEAR * INNER), (me >> 1) & 1, ((me >> 2) & 1) * 2 + (me & 1)


def layer_steps(n_far):
    return [0, 1, *range(n_far * NEAR - 1, 1, -1)]


def layer_partner(far, near, n_far, k):
    return partner(far, n_far, k // NEAR) * NEAR + partner(near, NEAR, k % NEAR)


def swap(sends, to):
    pairs = [[(i, to(i, k)) for i in range(lax.axis_size("dst"))] for k in range(len(sends) + 1)]
    return [lax.ppermute(x, "dst", pairs[k + 1]) for k, x in enumerate(sends)]


def prepare(
    off_in, cnt_in, rel_in, sid_in, attr_in, cot_in, feat_in, bias_in, w_node_in, w_edge_in, w_out_in,
    rows_out, dst_out, turned_out, src_out, cot_out, feat_out, bias_out, w_node_out, w_edge_out,
    w_out_out, off, cnt, rel, sid, sems,
):
    width = attr_in.shape[1]
    copies = load(
        [(off_in, off), (cnt_in, cnt), (rel_in, rel), (sid_in, sid)]
        + [(attr_in, rows_out.at[:, :width]), (cot_in, cot_out)]
        + [(feat_in, feat_out), (bias_in, bias_out)]
        + [(w_edge_in, w_edge_out), (w_node_in, w_node_out), (w_out_in, w_out_out)],
        sems,
    )
    wait(copies[:4])
    spare = rows_out.shape[1] - width - PARTS * src_out.shape[0]
    fill = [jnp.zeros((spare, rel.shape[1]), F32)] if spare else []
    for at, to_dst, to_src in edge_hots(off, cnt, rel, sid, dst_out.shape[0], src_out.shape[0]):
        dst_out[:, at] = to_dst.astype(BF16)
        turned_out[at, :] = to_dst.T.astype(BF16)
        src_out[:, at] = to_src.astype(BF16)
        rows_out[at, width:] = jnp.concatenate([to_src] * PARTS + fill, axis=0).T.astype(BF16)
    wait(copies[4:])


def forward(n_src, rows, dst_hot, bias, w_node, w_edge, w_out, *refs):
    feats, (half_out, sums_out, group, first, hidden) = refs[:n_src], refs[n_src:]
    me, owned = lax.axis_index("src"), feats[0].shape[0]
    for k, ref in enumerate(feats):
        group[part(lax.rem(me + k, n_src), owned), :] = ref[...]
    table = 0.5 * (dot(group[...], w_node[...]) + bias[...])
    first[: w_edge.shape[0], :] = 0.5 * w_edge[...]
    end = w_edge.shape[0]
    for _ in range(PARTS):
        piece = table.astype(BF16)
        first[end : end + group.shape[0], :] = piece
        table = table - piece.astype(F32)
        end += group.shape[0]
    if first.shape[0] > end:
        first[end:, :] = jnp.zeros_like(first[end:, :])
    for c in chunks(rows.shape[0]):
        half = dot(rows[c, :], first[...])
        half_out[c, :] = half
        hidden[c, :] = (half * jnp.tanh(half) + half).astype(BF16)
    high, low = halves(dot(dst_hot[...], hidden[...]))
    sums_out[...] = dot(high, w_out[...]) + dot(low, w_out[...])


def pack(n_far, owned, sums, *refs):
    parts, (cots_out, keep, *sends) = refs[:n_far], refs[n_far:]
    far, near, me = here()
    for k, ref in enumerate(parts):
        cots_out[part(partner(far, n_far, k, True), owned), :] = ref[...]
    rows = keep.shape[0]
    for k, out in enumerate([keep, *sends]):
        to = partner(me, INNER, STEPS[k])
        for z in range(n_far * NEAR):
            whose = jnp.where(z == far * NEAR + near, to, to ^ 1)
            its = sums[part(block(z // NEAR, z % NEAR, whose), owned), :]
            out[z * owned : (z + 1) * owned, :] = its.astype(out.dtype)
        if k:
            out[rows:, :] = cots_out[...]


def spread(n_far, owned, _, cots, keep, *refs):
    parts, (cots_out, own, *sends, total) = refs[: INNER - 1], refs[INNER - 1 :]
    far, near, me = here()
    rows = keep.shape[0]
    for k, ref in enumerate([cots] + [ref.at[rows:, :] for ref in parts]):
        owner = partner(me, INNER, STEPS[k], True)
        for f in range(n_far):
            whose = jnp.where(f == far, owner, owner ^ 1)
            cots_out[part(f * INNER + whose, owned), :] = ref[f * owned : (f + 1) * owned, :]
    total[...] = sum((ref[:rows, :].astype(F32) for ref in parts), keep[...])
    for k, out in enumerate([own, *sends]):
        layer = layer_partner(far, near, n_far, layer_steps(n_far)[k])
        out[:owned, :] = total[part(layer, owned), :].astype(out.dtype)
    sends[0][owned:, :] = cots_out[...]


def slopes(_, half, w_node, w_out, slope_out, w_node_out, w_out_out):
    w_out_out[...] = w_out[...].T
    turned = w_node[...].T
    w_node_out[...] = jnp.concatenate([turned, turned], axis=0)
    for c in chunks(half.shape[0]):
        t = jnp.tanh(half[c, :])
        slope_out[c, :] = 0.5 + 0.5 * (t + half[c, :] * (1.0 - t * t))


def backward(
    n_src, slope, dst_hot, src_hot, w_node, w_out, cots_near, came,
    d_pre, keep_out, send_out, total, cots,
):
    _, near, _ = here()
    owned, run = keep_out.shape[0], 2 * keep_out.shape[0]
    for pair in range(cots_near.shape[0] // run):
        at = pair * run
        cots[part(pair * NEAR + near, run), :] = cots_near[at : at + run, :]
        at += owned
        cots[part(pair * NEAR + 1 - near, run), :] = came[at : at + run, :]
    for c in chunks(slope.shape[0]):
        d_message = dot(dst_hot[c, :], cots[...]).astype(BF16)
        d_pre[c, :] = (dot(d_message, w_out[...]) * slope[c, :]).astype(BF16)
    parts = jnp.concatenate(halves(dot(src_hot[...], d_pre[...])), axis=1)
    total[...] = dot(parts, w_node[...])
    me = lax.axis_index("src")
    keep_out[...] = total[part(me, owned), :]
    for k in range(1, n_src):
        send_out[k - 1] = total[part(lax.rem(me + k, n_src), owned), :].astype(BF16)


def attributes(d_pre, w_edge, attr_out):
    for c in chunks(d_pre.shape[0]):
        attr_out[c, :] = dot(d_pre[c, :], w_edge[...], NT).astype(BF16)


def finish(n_agg, *refs):
    agg_out, grads_out = refs[-2:]
    owned = agg_out.shape[0]
    agg_out[...] = sum(ref[:owned, :].astype(F32) for ref in refs[:n_agg]).astype(BF16)
    grads_out[...] = sum(ref[...].astype(F32) for ref in refs[n_agg:-2]).astype(BF16)


def ahead(x, axis, k):
    n = lax.axis_size(axis)
    return lax.ppermute(x, axis, [((i + k) % n, i) for i in range(n)])


def local(
    node_feats, cotangent, edge_attr, src_ids, dst_rel, offsets, counts, w_node, w_edge, bias, w_out
):
    edges, attr_width = edge_attr.shape
    blocks = offsets.shape[0]
    width = edges // blocks
    owned, feat = node_feats.shape
    hidden = w_node.shape[1]
    n_src, n_dst = lax.axis_size("src"), lax.axis_size("dst")
    dst_rows, src_rows = owned * n_dst, owned * n_src
    n_far = n_dst // (NEAR * INNER)
    layers = n_far * NEAR
    params = pltpu.CompilerParams(vmem_limit_bytes=32 * 2**20)

    def array(*shape, dtype=BF16):
        return jax.ShapeDtypeStruct(shape, dtype)

    def rows_of(blocks, dtype=BF16):
        return array(blocks * owned, feat, dtype=dtype)

    def in_hbm(x):
        return pltpu.with_memory_space_constraint(x, pltpu.HBM)

    def call(kernel, name, args, outs, scratch=(), specs=None):
        return pl.pallas_call(
            kernel,
            name=name,
            in_specs=specs or [VMEM] * len(args),
            out_specs=[VMEM] * len(outs),
            out_shape=outs,
            scratch_shapes=list(scratch),
            compiler_params=params,
        )(*args)

    ints = [offsets, counts, dst_rel.reshape(blocks, width), src_ids.reshape(blocks, width)]
    bias = bias.reshape(1, hidden)
    feats = [ahead(node_feats, "src", k) for k in range(1, n_src)]
    depth = attr_width + PARTS * src_rows
    depth += -depth % 128

    rows, dst_hot, turned, src_hot, cots, own, *params_near = call(
        prepare,
        "prepare",
        [in_hbm(x) for x in (*ints, edge_attr, cotangent, node_feats, bias, w_node, w_edge, w_out)],
        [
            array(edges, depth),
            array(dst_rows, edges),
            array(edges, dst_rows),
            array(src_rows, edges),
            rows_of(1),
            rows_of(1),
            array(*bias.shape, dtype=F32),
        ]
        + [array(*x.shape) for x in (w_node, w_edge, w_out)],
        [pltpu.SMEM(x.shape, jnp.int32) for x in ints[:2]]
        + [pltpu.VMEM(x.shape, jnp.int32) for x in ints[2:]]
        + [pltpu.SemaphoreType.DMA((11,))],
        [ANY] * 11,
    )
    _, w_node, w_edge, w_out = params_near

    def to_far(i, k):
        far, near, me = place(i)
        return block(partner_of(far, n_far, k), near, me ^ 1)

    parts = swap([cotangent] * (n_far - 1), to_far)

    half, sums = call(
        lambda *refs: forward(n_src, *refs),
        "forward",
        [rows, dst_hot, *params_near, own, *feats],
        [array(edges, hidden, dtype=F32), rows_of(n_dst, F32)],
        [
            pltpu.VMEM((src_rows, feat), BF16),
            pltpu.VMEM((depth, hidden), BF16),
            pltpu.VMEM((edges, hidden), BF16),
        ],
    )

    cots, keep, *sends = call(
        lambda *refs: pack(n_far, owned, *refs),
        "pack",
        [sums, cots, *parts],
        [rows_of(n_far), rows_of(layers, F32)] + [rows_of(layers + n_far)] * (INNER - 1),
    )
    def to_inner(i, k):
        far, near, me = place(i)
        return block(far, near, partner_of(me, INNER, STEPS[k]))

    parts = swap(sends, to_inner)

    slope, w_node, w_out = call(
        slopes,
        "slopes",
        [keep, half, w_node, w_out],
        [array(edges, hidden, dtype=F32), array(2 * hidden, feat), array(*w_out.shape[::-1])],
    )

    beside = n_far * INNER
    cots, keep, *sends = call(
        lambda *refs: spread(n_far, owned, *refs),
        "spread",
        [slope, cots, keep, *parts],
        [rows_of(beside), rows_of(1, F32), rows_of(1 + beside)] + [rows_of(1, F32)] * (layers - 2),
        [pltpu.VMEM((layers * owned, feat), F32)],
        [ANY] + [VMEM] * (1 + INNER),
    )

    def to_layer(i, k):
        far, near, me = place(i)
        k = layer_steps(n_far)[k]
        far, near = partner_of(far, n_far, k // NEAR), partner_of(near, NEAR, k % NEAR)
        return block(far, near, me ^ 1)

    parts = swap(sends, to_layer)

    d_pre, keep_grads, send_grads = call(
        lambda *refs: backward(n_src, *refs),
        "backward",
        [slope, turned, src_hot, w_node, w_out, cots, parts[0]],
        [array(edges, hidden), rows_of(1, F32), array(n_src - 1, owned, feat)],
        [pltpu.VMEM((src_rows, feat), F32), pltpu.VMEM((dst_rows, feat), BF16)],
    )

    others = [ahead(send_grads[k - 1], "src", n_src - k) for k in range(1, n_src)]

    (attr_grads,) = call(
        attributes,
        "attributes",
        [d_pre, w_edge],
        [array(edges, attr_width)],
    )

    aggregated, node_grads = call(
        lambda *refs: finish(1 + len(parts), *refs),
        "finish",
        [keep, *parts, keep_grads, *others],
        [rows_of(1), rows_of(1)],
    )
    return aggregated, node_grads, attr_grads


def solution(mesh):
    in_specs = (
        P(("dst", "src"), None),
        P(("src", "dst"), None),
        P(("src", "dst"), None),
        P(("src", "dst")),
        P(("src", "dst")),
        P(("src", "dst")),
        P(("src", "dst")),
        P(),
        P(),
        P(),
        P(),
    )
    out_specs = (P(("src", "dst"), None), P(("dst", "src"), None), P(("src", "dst"), None))
    return jax.shard_map(local, mesh=mesh, in_specs=in_specs, out_specs=out_specs, check_vma=False)
```

```python
import math

import jax
import jax.numpy as jnp
from jax import lax
from jax.experimental import pallas as pl
from jax.experimental.pallas import tpu as pltpu
from jax.sharding import PartitionSpec as P

F32 = jnp.float32
BF16 = jnp.bfloat16
NN = (((1,), (0,)), ((), ()))
NT = (((1,), (1,)), ((), ()))
TN = (((0,), (0,)), ((), ()))
SMEM = pl.BlockSpec(memory_space=pltpu.SMEM)
VMEM = pl.BlockSpec(memory_space=pltpu.VMEM)
ANY = pl.BlockSpec(memory_space=pl.ANY)
CHUNK = 1536
PARTS = 3


def dot(a, b, dims=NN):
    return lax.dot_general(a, b, dims, preferred_element_type=F32)


def halves(x):
    high = x.astype(BF16)
    return high, (x - high.astype(F32)).astype(BF16)


def chunks(edges):
    return [pl.ds(c, min(CHUNK, edges - c)) for c in range(0, edges, CHUNK)]


def load(pairs, sems):
    copies = [pltpu.make_async_copy(*pair, sems.at[i]) for i, pair in enumerate(pairs)]
    for copy in copies:
        copy.start()
    return copies


def wait(copies):
    for copy in copies:
        copy.wait()


def edge_hots(off, cnt, rel, sid, dst_rows, src_rows):
    blocks, width = rel.shape
    lane = lax.broadcasted_iota(jnp.int32, (1, width), 1)
    dst_row = lax.broadcasted_iota(jnp.int32, (dst_rows, width), 0)
    src_row = lax.broadcasted_iota(jnp.int32, (src_rows, width), 0)
    for b in range(blocks):
        target = jnp.where(lane < cnt[b], rel[b : b + 1, :] + off[b], -1)
        to_dst = (dst_row == target).astype(F32)
        to_src = (src_row == sid[b : b + 1, :]).astype(F32)
        yield pl.ds(b * width, width), to_dst, to_src


def partner(me, n, k, back=False):
    if n & (n - 1) == 0:
        return me ^ k
    return lax.rem(me + (n - k if back else k), n)


def partner_of(me, n, k):
    return me ^ k if n & (n - 1) == 0 else (me + k) % n


def part(index, rows):
    return pl.ds(pl.multiple_of(index * rows, rows), rows)


INNER, NEAR = 4, 2
STEPS = (0, 2, 3, 1)


def block(far, near, me):
    return far * (NEAR * INNER) + (me >> 1) * 4 + near * 2 + (me & 1)


def place(index):
    return index // (NEAR * INNER), (index >> 1) & 1, ((index >> 2) & 1) * 2 + (index & 1)


def here():
    me = lax.axis_index("dst")
    return lax.div(me, NEAR * INNER), (me >> 1) & 1, ((me >> 2) & 1) * 2 + (me & 1)


def layer_steps(n_far):
    return [0, 1, *range(n_far * NEAR - 1, 1, -1)]


def layer_partner(far, near, n_far, k):
    return partner(far, n_far, k // NEAR) * NEAR + partner(near, NEAR, k % NEAR)


def swap(sends, to):
    pairs = [[(i, to(i, k)) for i in range(lax.axis_size("dst"))] for k in range(len(sends) + 1)]
    return [lax.ppermute(x, "dst", pairs[k + 1]) for k, x in enumerate(sends)]


def prepare(
    off_in, cnt_in, rel_in, sid_in, attr_in, cot_in, feat_in, bias_in, w_node_in, w_edge_in, w_out_in,
    rows_out, dst_out, src_out, cot_out, feat_out, bias_out, w_node_out, w_edge_out,
    w_out_out, off, cnt, rel, sid, sems,
):
    width = attr_in.shape[1]
    copies = load(
        [(off_in, off), (cnt_in, cnt), (rel_in, rel), (sid_in, sid)]
        + [(attr_in, rows_out.at[:, :width]), (cot_in, cot_out)]
        + [(feat_in, feat_out), (bias_in, bias_out)]
        + [(w_edge_in, w_edge_out), (w_node_in, w_node_out), (w_out_in, w_out_out)],
        sems,
    )
    wait(copies[:4])
    spare = rows_out.shape[1] - width - PARTS * src_out.shape[0]
    fill = [jnp.zeros((spare, rel.shape[1]), F32)] if spare else []
    for at, to_dst, to_src in edge_hots(off, cnt, rel, sid, dst_out.shape[0], src_out.shape[0]):
        dst_out[:, at] = to_dst.astype(BF16)
        src_out[:, at] = to_src.astype(BF16)
        rows_out[at, width:] = jnp.concatenate([to_src] * PARTS + fill, axis=0).T.astype(BF16)
    wait(copies[4:])


def forward(n_src, rows, dst_hot, bias, w_node, w_edge, w_out, *refs):
    feats, (half_out, sums_out, group, first, hidden) = refs[:n_src], refs[n_src:]
    me, owned = lax.axis_index("src"), feats[0].shape[0]
    for k, ref in enumerate(feats):
        group[part(lax.rem(me + k, n_src), owned), :] = ref[...]
    table = 0.5 * (dot(group[...], w_node[...]) + bias[...])
    first[: w_edge.shape[0], :] = 0.5 * w_edge[...]
    end = w_edge.shape[0]
    for _ in range(PARTS):
        piece = table.astype(BF16)
        first[end : end + group.shape[0], :] = piece
        table = table - piece.astype(F32)
        end += group.shape[0]
    if first.shape[0] > end:
        first[end:, :] = jnp.zeros_like(first[end:, :])
    for c in chunks(rows.shape[0]):
        half = dot(rows[c, :], first[...])
        half_out[c, :] = half
        hidden[c, :] = (half * jnp.tanh(half) + half).astype(BF16)
    high, low = halves(dot(dst_hot[...], hidden[...]))
    sums_out[...] = dot(high, w_out[...]) + dot(low, w_out[...])


def pack(n_far, owned, sums, *refs):
    parts, (cots_out, keep, *sends) = refs[:n_far], refs[n_far:]
    far, near, me = here()
    for k, ref in enumerate(parts):
        cots_out[part(partner(far, n_far, k, True), owned), :] = ref[...]
    rows = keep.shape[0]
    for k, out in enumerate([keep, *sends]):
        to = partner(me, INNER, STEPS[k])
        for z in range(n_far * NEAR):
            whose = jnp.where(z == far * NEAR + near, to, to ^ 1)
            its = sums[part(block(z // NEAR, z % NEAR, whose), owned), :]
            out[z * owned : (z + 1) * owned, :] = its.astype(out.dtype)
        if k:
            out[rows:, :] = cots_out[...]


def spread(n_far, owned, _, cots, keep, *refs):
    parts, (cots_out, own, *sends, total) = refs[: INNER - 1], refs[INNER - 1 :]
    far, near, me = here()
    rows = keep.shape[0]
    for k, ref in enumerate([cots] + [ref.at[rows:, :] for ref in parts]):
        owner = partner(me, INNER, STEPS[k], True)
        for f in range(n_far):
            whose = jnp.where(f == far, owner, owner ^ 1)
            cots_out[part(f * INNER + whose, owned), :] = ref[f * owned : (f + 1) * owned, :]
    total[...] = sum((ref[:rows, :].astype(F32) for ref in parts), keep[...])
    for k, out in enumerate([own, *sends]):
        layer = layer_partner(far, near, n_far, layer_steps(n_far)[k])
        out[:owned, :] = total[part(layer, owned), :].astype(out.dtype)
    sends[0][owned:, :] = cots_out[...]


def slopes(_, half, w_node, w_out, dst_hot, slope_out, w_node_out, w_out_out, turned_out):
    for c in range(0, half.shape[0], 512):
        turned_out[c : c + 512, :] = dst_hot[:, c : c + 512].astype(F32).T.astype(BF16)
    w_out_out[...] = w_out[...].T
    w_node_out[...] = w_node[...].T
    for c in chunks(half.shape[0]):
        t = jnp.tanh(half[c, :])
        slope_out[c, :] = 0.5 + 0.5 * (t + half[c, :] * (1.0 - t * t))


def backward(
    n_src, slope, dst_hot, src_hot, w_node, w_out, cots_near, came,
    d_pre, keep_out, send_out, total, cots,
):
    _, near, _ = here()
    owned, run = keep_out.shape[0], 2 * keep_out.shape[0]
    for pair in range(cots_near.shape[0] // run):
        at = pair * run
        cots[part(pair * NEAR + near, run), :] = cots_near[at : at + run, :]
        at += owned
        cots[part(pair * NEAR + 1 - near, run), :] = came[at : at + run, :]
    for c in chunks(slope.shape[0]):
        d_message = dot(dst_hot[c, :], cots[...]).astype(BF16)
        d_pre[c, :] = (dot(d_message, w_out[...]) * slope[c, :]).astype(BF16)
    high, low = halves(dot(src_hot[...], d_pre[...]))
    total[...] = dot(high, w_node[...]) + dot(low, w_node[...])
    me = lax.axis_index("src")
    keep_out[...] = total[part(me, owned), :]
    for k in range(1, n_src):
        send_out[k - 1] = total[part(lax.rem(me + k, n_src), owned), :].astype(BF16)


def attributes(d_pre, w_edge, attr_out):
    for c in chunks(d_pre.shape[0]):
        attr_out[c, :] = dot(d_pre[c, :], w_edge[...], NT).astype(BF16)


def finish(n_agg, *refs):
    agg_out, grads_out = refs[-2:]
    owned = agg_out.shape[0]
    agg_out[...] = sum(ref[:owned, :].astype(F32) for ref in refs[:n_agg]).astype(BF16)
    grads_out[...] = sum(ref[...].astype(F32) for ref in refs[n_agg:-2]).astype(BF16)


def ahead(x, axis, k):
    n = lax.axis_size(axis)
    return lax.ppermute(x, axis, [((i + k) % n, i) for i in range(n)])


def local(
    node_feats, cotangent, edge_attr, src_ids, dst_rel, offsets, counts, w_node, w_edge, bias, w_out
):
    edges, attr_width = edge_attr.shape
    blocks = offsets.shape[0]
    width = edges // blocks
    owned, feat = node_feats.shape
    hidden = w_node.shape[1]
    n_src, n_dst = lax.axis_size("src"), lax.axis_size("dst")
    dst_rows, src_rows = owned * n_dst, owned * n_src
    n_far = n_dst // (NEAR * INNER)
    layers = n_far * NEAR
    params = pltpu.CompilerParams(vmem_limit_bytes=32 * 2**20)

    def array(*shape, dtype=BF16):
        return jax.ShapeDtypeStruct(shape, dtype)

    def rows_of(blocks, dtype=BF16):
        return array(blocks * owned, feat, dtype=dtype)

    def in_hbm(x):
        return pltpu.with_memory_space_constraint(x, pltpu.HBM)

    def call(kernel, name, args, outs, scratch=(), specs=None):
        return pl.pallas_call(
            kernel,
            name=name,
            in_specs=specs or [VMEM] * len(args),
            out_specs=[VMEM] * len(outs),
            out_shape=outs,
            scratch_shapes=list(scratch),
            compiler_params=params,
        )(*args)

    ints = [offsets, counts, dst_rel.reshape(blocks, width), src_ids.reshape(blocks, width)]
    bias = bias.reshape(1, hidden)
    feats = [ahead(node_feats, "src", k) for k in range(1, n_src)]
    depth = attr_width + PARTS * src_rows
    depth += -depth % 128

    rows, dst_hot, src_hot, cots, own, *params_near = call(
        prepare,
        "prepare",
        [in_hbm(x) for x in (*ints, edge_attr, cotangent, node_feats, bias, w_node, w_edge, w_out)],
        [
            array(edges, depth),
            array(dst_rows, edges),
            array(src_rows, edges),
            rows_of(1),
            rows_of(1),
            array(*bias.shape, dtype=F32),
        ]
        + [array(*x.shape) for x in (w_node, w_edge, w_out)],
        [pltpu.SMEM(x.shape, jnp.int32) for x in ints[:2]]
        + [pltpu.VMEM(x.shape, jnp.int32) for x in ints[2:]]
        + [pltpu.SemaphoreType.DMA((11,))],
        [ANY] * 11,
    )
    _, w_node, w_edge, w_out = params_near

    def to_far(i, k):
        far, near, me = place(i)
        return block(partner_of(far, n_far, k), near, me ^ 1)

    parts = swap([cotangent] * (n_far - 1), to_far)

    half, sums = call(
        lambda *refs: forward(n_src, *refs),
        "forward",
        [rows, dst_hot, *params_near, own, *feats],
        [array(edges, hidden, dtype=F32), rows_of(n_dst, F32)],
        [
            pltpu.VMEM((src_rows, feat), BF16),
            pltpu.VMEM((depth, hidden), BF16),
            pltpu.VMEM((edges, hidden), BF16),
        ],
    )

    cots, keep, *sends = call(
        lambda *refs: pack(n_far, owned, *refs),
        "pack",
        [sums, cots, *parts],
        [rows_of(n_far), rows_of(layers, F32)] + [rows_of(layers + n_far)] * (INNER - 1),
    )
    def to_inner(i, k):
        far, near, me = place(i)
        return block(far, near, partner_of(me, INNER, STEPS[k]))

    parts = swap(sends, to_inner)

    slope, w_node, w_out, turned = call(
        slopes,
        "slopes",
        [keep, half, w_node, w_out, dst_hot],
        [array(edges, hidden, dtype=F32)]
        + [array(*x.shape[::-1]) for x in (w_node, w_out, dst_hot)],
    )

    beside = n_far * INNER
    cots, keep, *sends = call(
        lambda *refs: spread(n_far, owned, *refs),
        "spread",
        [slope, cots, keep, *parts],
        [rows_of(beside), rows_of(1, F32), rows_of(1 + beside)] + [rows_of(1, F32)] * (layers - 2),
        [pltpu.VMEM((layers * owned, feat), F32)],
        [ANY] + [VMEM] * (1 + INNER),
    )

    def to_layer(i, k):
        far, near, me = place(i)
        k = layer_steps(n_far)[k]
        far, near = partner_of(far, n_far, k // NEAR), partner_of(near, NEAR, k % NEAR)
        return block(far, near, me ^ 1)

    parts = swap(sends, to_layer)

    d_pre, keep_grads, send_grads = call(
        lambda *refs: backward(n_src, *refs),
        "backward",
        [slope, turned, src_hot, w_node, w_out, cots, parts[0]],
        [array(edges, hidden), rows_of(1, F32), array(n_src - 1, owned, feat)],
        [pltpu.VMEM((src_rows, feat), F32), pltpu.VMEM((dst_rows, feat), BF16)],
    )

    others = [ahead(send_grads[k - 1], "src", n_src - k) for k in range(1, n_src)]

    (attr_grads,) = call(
        attributes,
        "attributes",
        [d_pre, w_edge],
        [array(edges, attr_width)],
    )

    aggregated, node_grads = call(
        lambda *refs: finish(1 + len(parts), *refs),
        "finish",
        [keep, *parts, keep_grads, *others],
        [rows_of(1), rows_of(1)],
    )
    return aggregated, node_grads, attr_grads


def solution(mesh):
    in_specs = (
        P(("dst", "src"), None),
        P(("src", "dst"), None),
        P(("src", "dst"), None),
        P(("src", "dst")),
        P(("src", "dst")),
        P(("src", "dst")),
        P(("src", "dst")),
        P(),
        P(),
        P(),
        P(),
    )
    out_specs = (P(("src", "dst"), None), P(("dst", "src"), None), P(("src", "dst"), None))
    return jax.shard_map(local, mesh=mesh, in_specs=in_specs, out_specs=out_specs, check_vma=False)
```
